32 devices in a mesh: groups: 1, tm: 8 (over z, core), dp: 4 (over y, x).
Axes of the slice: x: 2, y: 2, z: 4, core: 2. Of those that a mesh axis runs over, the one named last changes fastest.
Arguments:
- queries: bfloat16 [4, 2048, 1024], P(('groups', 'dp'), 'tm'), may hold values from -6.4 to 6.4
- keys: bfloat16 [4, 2048, 1024], P(('groups', 'dp'), 'tm'), may hold values from -8.8 to 8.8
- values: bfloat16 [4, 2048, 1024], P(('groups', 'dp'), 'tm'), may hold values from -6 to 6
- lengths: int32 [4], P(('groups', 'dp')), may hold values from 128 to 2048, as said below
- out_weight: bfloat16 [1024, 1024], P('dp'), may hold values from -0.1875 to 0.1875
- grad_out: bfloat16 [4, 2048, 1024], P(('groups', 'dp'), 'tm'), may hold values from -6 to 6
Outputs:
- attended: bfloat16 [4, 2048, 1024], P(('groups', 'dp'), 'tm')
- grad_queries: bfloat16 [4, 2048, 1024], P(('groups', 'dp'), 'tm')
- grad_keys: bfloat16 [4, 2048, 1024], P(('groups', 'dp'), 'tm')
- grad_values: bfloat16 [4, 2048, 1024], P(('groups', 'dp'), 'tm')
- grad_weight: float32 [1024, 1024], P(('groups', 'dp'))
The draws below stay inside these ranges and needn't reach their ends.
Inputs may be any that keep to these rules, and one draw needn't show every extreme that they name: `lengths`: in every draw one utterance of a part fills all 2048 frames and another has exactly 128 valid frames.
All inputs are finite; a program needn't handle non-finite values.
Results may differ from the reference program's by a relative error of at most 0.0069.
Values may be sent and summed in bfloat16 or wider, within the bound.
A program may use at most 128 MiB of HBM per device.

```python
import math
import jax
import jax.numpy as jnp
from jax import lax

D = 1024
H = 8
DH = 128
WIN = 128
F_DEV = 256
FRAMES = 2048
UTTS = 4
N_TM = 8


def paired_fields(key):
    shape = (UTTS, FRAMES, D)
    base = jax.random.fold_in(key, 17)
    key_q, key_k, scale_q, scale_k = jax.random.split(base, 4)
    rows_q = jnp.exp(jax.random.uniform(scale_q, (UTTS, FRAMES, 1), minval=math.log(0.35), maxval=math.log(1.6)))
    rows_k = jnp.exp(jax.random.uniform(scale_k, (UTTS, FRAMES, 1), minval=math.log(0.35), maxval=math.log(2.2)))
    field_q = jax.random.truncated_normal(key_q, -4.0, 4.0, shape) * rows_q
    field_k = jax.random.truncated_normal(key_k, -4.0, 4.0, shape) * rows_k
    return (field_q, field_k)


def draw_queries(key, part):
    return paired_fields(key)[0].astype(jnp.bfloat16)


def draw_keys(key, part):
    return paired_fields(key)[1].astype(jnp.bfloat16)


def draw_lengths(key, part):
    key_a, key_b, key_c = jax.random.split(jax.random.fold_in(key, 29), 3)
    lowest = FRAMES // 16
    drawn = jax.random.randint(key_a, (UTTS,), lowest, FRAMES + 1)
    longest = jax.random.randint(key_b, (), 0, UTTS)
    shortest = (longest + 1 + jax.random.randint(key_c, (), 0, UTTS - 1)) % UTTS
    spots = jnp.arange(UTTS)
    drawn = jnp.where(spots == longest, FRAMES, drawn)
    drawn = jnp.where(spots == shortest, lowest, drawn)
    return drawn.astype(jnp.int32)


def block_levels(rng, shape, shards, low, top_value):
    def one(dim, shards_of):
        draws = jax.random.uniform(jax.random.fold_in(jax.random.fold_in(rng, 6), dim), (shards_of,), jnp.float32, low / len(shards), top_value / len(shards))
        return jnp.repeat(jnp.exp(draws), shape[dim] // shards_of).reshape((-1,) + (1,) * (len(shape) - dim - 1))

    level = one(*shards[0])
    for cut in shards[1:]:
        level = level * one(*cut)
    return level


def gaussian(stream_key, dims, spread, limit, pieces=(), held_as=jnp.bfloat16):
    values = spread * jax.random.normal(stream_key, dims, jnp.float32)
    if pieces:
        values = values * block_levels(stream_key, dims, pieces, -0.22, 0.18)
    return jnp.clip(values, -limit, limit).astype(held_as)


def setup_inputs(seed: int = 0, part: int = 0) -> dict:
    key_list = jax.random.split(jax.random.key(seed), 7)
    part_keys = jax.random.split(jax.random.fold_in(key_list[6], part), 7)
    return {
        "queries": draw_queries(jax.random.fold_in(jax.random.fold_in(key_list[6], part), 71), part),
        "keys": draw_keys(jax.random.fold_in(jax.random.fold_in(key_list[6], part), 71), part),
        "values": gaussian(part_keys[2], (UTTS, FRAMES, D), 1.0, 6.0, ((0, 4), (1, 8))),
        "lengths": draw_lengths(jax.random.fold_in(jax.random.fold_in(key_list[6], part), 71), part),
        "out_weight": gaussian(key_list[4], (D, D), D ** -0.5, 0.1875, ((0, 4),)),
        "grad_out": gaussian(part_keys[5], (UTTS, FRAMES, D), 1.0, 6.0, ((0, 4), (1, 8))),
    }


NEG_FILL = -1000000000.0

def split_heads(array):
    return array.reshape(array.shape[0], H, DH).astype(jnp.float32)

def window_mask(query_pos, key_pos, length):
    near = jnp.abs(query_pos[:, None] - key_pos[None, :]) <= WIN
    live_keys = (key_pos[None, :] >= 0) & (key_pos[None, :] < length)
    live_rows = (query_pos[:, None] >= 0) & (query_pos[:, None] < length)
    return near & live_keys & live_rows

def normalize(scores, allowed):
    masked = jnp.where(allowed[None], scores, NEG_FILL)
    top = lax.optimization_barrier(jnp.max(masked, axis=-1, keepdims=True))
    total = lax.optimization_barrier(jnp.sum(jnp.exp(masked - top), axis=-1, keepdims=True))
    log_total = top + jnp.log(total)
    probs_f = jnp.exp(jnp.where(allowed[None], scores - log_total, NEG_FILL))
    return (log_total[..., 0], probs_f)

def reference(queries, keys, values, lengths, out_weight, grad_out):
    scale = 1.0 / math.sqrt(DH)
    inv_count = 1.0 / math.sqrt(UTTS * FRAMES)
    span = F_DEV + 2 * WIN

    def one_utterance(items):
        query_rows, key_rows, value_rows, grad_rows, length = items
        pad_keys = jnp.pad(key_rows, ((WIN, WIN), (0, 0)))
        pad_values = jnp.pad(value_rows, ((WIN, WIN), (0, 0)))

        def first_pass(block):
            start = (block * F_DEV).astype(jnp.int32)
            query_block = lax.dynamic_slice_in_dim(query_rows, start, F_DEV, 0)
            grad_block = lax.dynamic_slice_in_dim(grad_rows, start, F_DEV, 0)
            key_block = lax.dynamic_slice_in_dim(pad_keys, start, span, 0)
            value_block = lax.dynamic_slice_in_dim(pad_values, start, span, 0)
            query_pos = start + jnp.arange(F_DEV, dtype=jnp.int32)
            key_pos = start - WIN + jnp.arange(span, dtype=jnp.int32)
            allowed = window_mask(query_pos, key_pos, length)
            scores = jnp.einsum('rhd,shd->hrs', split_heads(query_block), split_heads(key_block)) * scale
            log_total, probs_f = normalize(scores, allowed)
            probs = probs_f.astype(jnp.bfloat16)
            attn_out = jnp.einsum('hrs,shd->rhd', probs.astype(jnp.float32), split_heads(value_block))
            attn_out = attn_out.reshape(F_DEV, D).astype(jnp.bfloat16)
            valid = (query_pos < length)[:, None]
            attended = jnp.where(valid, jnp.dot(attn_out, out_weight, preferred_element_type=jnp.float32), 0.0)
            attended = attended.astype(jnp.bfloat16)
            masked_grad = jnp.where(valid, grad_block, jnp.zeros_like(grad_block))
            grad_attn = jnp.dot(masked_grad, out_weight.T, preferred_element_type=jnp.float32).astype(jnp.bfloat16)
            grad_probs = jnp.einsum('rhd,shd->hrs', split_heads(grad_attn), split_heads(value_block))
            row_delta = lax.optimization_barrier(jnp.sum(probs_f * grad_probs, axis=-1))
            grad_scores = (probs_f * (grad_probs - row_delta[..., None]) * scale).astype(jnp.bfloat16)
            grad_queries = jnp.einsum('hrs,shd->rhd', grad_scores.astype(jnp.float32), split_heads(key_block))
            grad_queries = grad_queries.reshape(F_DEV, D).astype(jnp.bfloat16)
            return (attended, attn_out, masked_grad, grad_attn, grad_queries, log_total, row_delta)
        firsts = lax.map(first_pass, jnp.arange(N_TM, dtype=jnp.int32))
        attended = firsts[0].reshape(FRAMES, D)
        attn_out = firsts[1].reshape(FRAMES, D)
        masked_grad = firsts[2].reshape(FRAMES, D)
        grad_attn = firsts[3].reshape(FRAMES, D)
        grad_queries = firsts[4].reshape(FRAMES, D)
        log_total = jnp.transpose(firsts[5], (1, 0, 2)).reshape(H, FRAMES)
        row_delta = jnp.transpose(firsts[6], (1, 0, 2)).reshape(H, FRAMES)
        weight_term = jnp.dot(attn_out.T, masked_grad, preferred_element_type=jnp.float32)
        pad_queries = jnp.pad(query_rows, ((WIN, WIN), (0, 0)))
        pad_grad = jnp.pad(grad_attn, ((WIN, WIN), (0, 0)))
        pad_total = jnp.pad(log_total, ((0, 0), (WIN, WIN)))
        pad_delta = jnp.pad(row_delta, ((0, 0), (WIN, WIN)))

        def second_pass(block):
            start = (block * F_DEV).astype(jnp.int32)
            key_block = lax.dynamic_slice_in_dim(key_rows, start, F_DEV, 0)
            value_block = lax.dynamic_slice_in_dim(value_rows, start, F_DEV, 0)
            query_block = lax.dynamic_slice_in_dim(pad_queries, start, span, 0)
            grad_block = lax.dynamic_slice_in_dim(pad_grad, start, span, 0)
            total_block = lax.dynamic_slice_in_dim(pad_total, start, span, 1)
            delta_block = lax.dynamic_slice_in_dim(pad_delta, start, span, 1)
            query_pos = start - WIN + jnp.arange(span, dtype=jnp.int32)
            key_pos = start + jnp.arange(F_DEV, dtype=jnp.int32)
            allowed = window_mask(query_pos, key_pos, length)
            scores = jnp.einsum('qhd,khd->hqk', split_heads(query_block), split_heads(key_block)) * scale
            probs_f = jnp.exp(jnp.where(allowed[None], scores - total_block[:, :, None], NEG_FILL))
            probs = probs_f.astype(jnp.bfloat16)
            grad_probs = jnp.einsum('qhd,khd->hqk', split_heads(grad_block), split_heads(value_block))
            grad_scores = (probs_f * (grad_probs - delta_block[:, :, None]) * scale).astype(jnp.bfloat16)
            grad_keys = jnp.einsum('hqk,qhd->khd', grad_scores.astype(jnp.float32), split_heads(query_block))
            grad_values = jnp.einsum('hqk,qhd->khd', probs.astype(jnp.float32), split_heads(grad_block))
            return (grad_keys.reshape(F_DEV, D).astype(jnp.bfloat16), grad_values.reshape(F_DEV, D).astype(jnp.bfloat16))
        seconds = lax.map(second_pass, jnp.arange(N_TM, dtype=jnp.int32))
        grad_keys = seconds[0].reshape(FRAMES, D)
        grad_values = seconds[1].reshape(FRAMES, D)
        return (attended, grad_queries, grad_keys, grad_values, weight_term)
    outs = lax.map(one_utterance, (queries, keys, values, grad_out, lengths))
    grad_weight = lax.optimization_barrier(jnp.sum(outs[4], axis=0)) * inv_count
    return (outs[0], outs[1], outs[2], outs[3], grad_weight)
```

```python
import functools
import math

import jax
import jax.numpy as jnp
from jax import lax
from jax.experimental import pallas as pl
from jax.experimental.pallas import tpu as pltpu
from jax.sharding import PartitionSpec as P

H = 8
WIN = 128
CHUNKS = 2
NEG_FILL = -1000000000.0
F32 = jnp.float32
BF16 = jnp.bfloat16


def dot(a, b, over_a, over_b):
    return lax.dot_general(a, b, (((over_a,), (over_b,)), ((), ())), preferred_element_type=F32)


def piece_grid(nz, shard, cols):
    down = min(nz, shard // 16)
    across = nz // down
    return down, across, shard // down, cols // across


def kernel(
    n_tm, n_dp, inv_count,
    len_ref, q_ref, k_hbm, v_hbm, w_hbm, g_ref,
    att_ref, dq_ref, dk_ref, dv_ref, gw_ref,
    kext, vext, wfull, gm, gsplit, gg, ao, ga, probs, mids, halo_out, halo_in,
    part_out, part_in, acc, z_own, z_out, z_in, final,
    own_sem, kv_send, kv_recv, w_send, w_recv, wf_send, wf_recv, g_send, g_recv,
    ao_send, ao_recv, h_send, h_recv, p_send, p_recv, z_send, z_recv,
    f_send, f_recv, x_send, x_recv,
):
    rows, width = q_ref.shape
    shard = width // n_dp
    half = shard // 2
    head = width // H
    heads = shard // head
    nz = n_tm // 2
    cols = width // 2
    ccols = cols // CHUNKS
    scale = 1.0 / math.sqrt(head)
    down, across, prow, pcol = piece_grid(nz, shard, ccols)

    tm = lax.axis_index("tm")
    dp = lax.axis_index("dp")
    z = tm // 2
    core = tm % 2
    partner = tm + 1 - 2 * core
    right = lax.rem(tm + 1, n_tm)
    left = lax.rem(tm + n_tm - 1, n_tm)
    has_left = tm > 0
    has_right = tm < n_tm - 1

    def peer(k):
        return lax.rem(dp + k, n_dp)

    def z_peer(k):
        return lax.rem(z + k, nz)

    def remote(src, dst, send, recv, **where):
        return pltpu.make_async_remote_copy(
            src_ref=src, dst_ref=dst, send_sem=send, recv_sem=recv,
            device_id=where, device_id_type=pl.DeviceIdType.MESH,
        )

    own = [
        pltpu.make_async_copy(k_hbm, kext.at[pl.ds(WIN, rows)], own_sem.at[0]),
        pltpu.make_async_copy(v_hbm, vext.at[pl.ds(WIN, rows)], own_sem.at[1]),
        pltpu.make_async_copy(w_hbm, wfull.at[dp], own_sem.at[2]),
    ]
    for copy in own:
        copy.start()

    barrier = pltpu.get_barrier_semaphore()
    for t in (left, right):
        pl.semaphore_signal(barrier, inc=1, device_id={"tm": t}, device_id_type=pl.DeviceIdType.MESH)
    for k in range(1, n_dp):
        pl.semaphore_signal(barrier, inc=1, device_id={"dp": peer(k)}, device_id_type=pl.DeviceIdType.MESH)
    for k in range(1, nz):
        pl.semaphore_signal(
            barrier, inc=1, device_id={"tm": 2 * z_peer(k) + core}, device_id_type=pl.DeviceIdType.MESH
        )
    pl.semaphore_wait(barrier, 2 + (n_dp - 1) + (nz - 1))

    to_right, to_left = [], []
    for i, (src, ext) in enumerate(((k_hbm, kext), (v_hbm, vext))):
        to_right.append(
            remote(src.at[pl.ds(rows - WIN, WIN)], ext.at[pl.ds(0, WIN)],
                   kv_send.at[0, i], kv_recv.at[0, i], tm=right)
        )
        to_left.append(
            remote(src.at[pl.ds(0, WIN)], ext.at[pl.ds(WIN + rows, WIN)],
                   kv_send.at[1, i], kv_recv.at[1, i], tm=left)
        )

    @pl.when(has_right)
    def _():
        for copy in to_right:
            copy.start()

    @pl.when(has_left)
    def _():
        for copy in to_left:
            copy.start()

    w_half = pl.ds(pl.multiple_of(core * half, half), half)
    w_copies = [
        remote(w_hbm.at[w_half], wfull.at[dp, w_half], w_send.at[k], w_recv.at[k], dp=peer(k + 1))
        for k in range(n_dp - 1)
    ]
    for copy in w_copies:
        copy.start()

    length = len_ref[0]
    start = tm * rows
    row_pos = start + lax.broadcasted_iota(jnp.int32, (rows, 1), 0)
    valid = row_pos < length
    masked_grad = jnp.where(valid, g_ref[...].astype(F32), 0.0).astype(BF16)
    gm[...] = masked_grad
    gsplit[0] = masked_grad[:, :cols]
    gsplit[1] = masked_grad[:, cols:]
    g_copy = remote(gsplit.at[1 - core], gg.at[pl.ds(rows, rows)], g_send, g_recv, tm=partner)
    g_copy.start()
    gg[pl.ds(0, rows), :] = gsplit[core]

    @pl.when(jnp.logical_not(has_left))
    def _():
        kext[pl.ds(0, WIN), :] = jnp.zeros((WIN, width), BF16)
        vext[pl.ds(0, WIN), :] = jnp.zeros((WIN, width), BF16)
        halo_in[:, 1] = jnp.zeros((n_dp, 2, WIN, shard), BF16)

    @pl.when(jnp.logical_not(has_right))
    def _():
        kext[pl.ds(WIN + rows, WIN), :] = jnp.zeros((WIN, width), BF16)
        vext[pl.ds(WIN + rows, WIN), :] = jnp.zeros((WIN, width), BF16)
        halo_in[:, 0] = jnp.zeros((n_dp, 2, WIN, shard), BF16)

    for copy in own:
        copy.wait()

    @pl.when(has_left)
    def _():
        for copy in to_right:
            copy.wait_recv()

    @pl.when(has_right)
    def _():
        for copy in to_left:
            copy.wait_recv()

    span = rows + 2 * WIN
    q_pos = start + lax.broadcasted_iota(jnp.int32, (rows, span), 0)
    k_pos = start - WIN + lax.broadcasted_iota(jnp.int32, (rows, span), 1)
    allowed = (jnp.abs(q_pos - k_pos) <= WIN) & (k_pos >= 0) & (k_pos < length)
    bias = jnp.where(allowed, 0.0, NEG_FILL)
    live = jnp.where(valid, 1.0, 0.0)

    def ao_copy(s):
        return remote(
            ao.at[s, pl.ds(0, rows)], ao.at[s, pl.ds(rows, rows)], ao_send.at[s], ao_recv.at[s], tm=partner
        )

    @pl.loop(0, n_dp)
    def _(s):
        at = pl.ds(pl.multiple_of(s * shard, shard), shard)
        q, k, v = q_ref[:, at], kext[:, at], vext[:, at]
        for i in range(heads):
            lanes = slice(i * head, (i + 1) * head)
            masked = dot(q[:, lanes], k[:, lanes], 1, 1) * scale + bias
            top = jnp.max(masked, axis=-1, keepdims=True)
            e = jnp.exp(masked - top)
            p = e * (live / jnp.sum(e, axis=-1, keepdims=True))
            probs[s * heads + i] = p
            ao[s, pl.ds(0, rows), lanes] = dot(p.astype(BF16), v[:, lanes], 1, 0).astype(BF16)
        ao_copy(s).start()

    def w_forward(k):
        src = lax.rem(dp + n_dp - 1 - k, n_dp)
        return remote(
            wfull.at[src, w_half], wfull.at[src, w_half], wf_send.at[k], wf_recv.at[k], tm=partner
        )

    for k in range(n_dp - 1):
        w_copies[k].wait_recv()
        w_forward(k).start()

    g_copy.wait_recv()
    for s in range(n_dp):
        ao_copy(s).wait_recv()

    def part_copy(c, k):
        return remote(
            part_out.at[c, k], part_in.at[c, k], p_send.at[c, k], p_recv.at[c, k], dp=peer(k + 1)
        )

    for c in range(CHUNKS):
        g_cols = gg[:, c * ccols:(c + 1) * ccols]
        for k in range(n_dp - 1):
            part_out[c, k] = dot(ao[peer(k + 1)], g_cols, 0, 0).astype(BF16)
            part_copy(c, k).start()
    for c in range(CHUNKS):
        acc[c] = dot(ao[dp], gg[:, c * ccols:(c + 1) * ccols], 0, 0)

    for k in range(n_dp - 1):
        w_forward(k).wait_recv()

    def halo_copy(s, side):
        return remote(
            halo_out.at[s, side], halo_in.at[s, side], h_send.at[s, side], h_recv.at[s, side],
            tm=(left, right)[side],
        )

    @pl.loop(0, n_dp)
    def _(s):
        at = pl.ds(pl.multiple_of(s * shard, shard), shard)
        q, k, v = q_ref[:, at], kext[:, at], vext[:, at]
        grad_attn = dot(gm[...], wfull[s], 1, 1).astype(BF16)
        for i in range(heads):
            lanes = slice(i * head, (i + 1) * head)
            p = probs[s * heads + i]
            grad_probs = dot(grad_attn[:, lanes], v[:, lanes], 1, 1)
            delta = jnp.sum(p * grad_probs, axis=-1, keepdims=True)
            grad_scores = (p * (grad_probs - delta) * scale).astype(BF16)
            hd = pl.ds(pl.multiple_of(s * shard + i * head, head), head)
            dq_ref[:, hd] = dot(grad_scores, k[:, lanes], 1, 0).astype(BF16)
            terms = (
                dot(grad_scores, q[:, lanes], 0, 0),
                dot(p.astype(BF16), grad_attn[:, lanes], 0, 0),
            )
            for which, term in enumerate(terms):
                halo_out[s, 0, which, :, lanes] = term[:WIN].astype(BF16)
                halo_out[s, 1, which, :, lanes] = term[WIN + rows:].astype(BF16)
                mids[which, :, hd] = term[WIN:WIN + rows]

        @pl.when(has_left)
        def _():
            halo_copy(s, 0).start()

        @pl.when(has_right)
        def _():
            halo_copy(s, 1).start()

    def z_copy(c, k):
        return remote(
            z_out.at[c, z_peer(k + 1)], z_in.at[c, k], z_send.at[c, k], z_recv.at[c, k],
            tm=2 * z_peer(k + 1) + core,
        )

    def final_copy(c, k):
        return remote(
            final.at[core, c, z], final.at[core, c, z], f_send.at[c, k], f_recv.at[c, k],
            tm=2 * z_peer(k + 1) + core,
        )

    def cross_copy(c):
        return remote(final.at[core, c], final.at[core, c], x_send.at[c], x_recv.at[c], tm=partner)

    def cut(j):
        r, a = (j // across) * prow, (j % across) * pcol
        return slice(r, r + prow), slice(a, a + pcol)

    def scatter(c):
        total = acc[c]
        for k in range(n_dp - 1):
            part_copy(c, k).wait_recv()
            total = total + part_in[c, k].astype(F32)
        for j in range(nz):
            r, a = cut(j)
            z_own[c, j] = total[r, a]
            z_out[c, j] = total[r, a].astype(BF16)
        for k in range(nz - 1):
            z_copy(c, k).start()

    def gather(c):
        total = z_own[c, z]
        for k in range(nz - 1):
            z_copy(c, k).wait_recv()
            total = total + z_in[c, k].astype(F32)
        final[core, c, z] = (total * inv_count).astype(BF16)
        for k in range(nz - 1):
            final_copy(c, k).start()

    def cross(c):
        for k in range(nz - 1):
            final_copy(c, k).wait_recv()
        cross_copy(c).start()

    for c in range(CHUNKS):
        scatter(c)

    attended = dot(ao[0, pl.ds(0, rows)], wfull[0], 1, 0)
    for s in range(1, n_dp):
        attended += dot(ao[s, pl.ds(0, rows)], wfull[s], 1, 0)
    att_ref[...] = jnp.where(valid, attended, 0.0).astype(BF16)

    for c in range(CHUNKS):
        gather(c)

    @pl.when(has_right)
    def _():
        for s in range(n_dp):
            halo_copy(s, 0).wait_recv()

    @pl.when(has_left)
    def _():
        for s in range(n_dp):
            halo_copy(s, 1).wait_recv()

    for which, out in enumerate((dk_ref, dv_ref)):
        for s in range(n_dp):
            lanes = slice(s * shard, (s + 1) * shard)
            out[0:WIN, lanes] = (
                mids[which, 0:WIN, lanes] + halo_in[s, 1, which].astype(F32)
            ).astype(BF16)
            if rows > 2 * WIN:
                out[WIN:rows - WIN, lanes] = mids[which, WIN:rows - WIN, lanes].astype(BF16)
            out[rows - WIN:rows, lanes] = (
                mids[which, rows - WIN:rows, lanes] + halo_in[s, 0, which].astype(F32)
            ).astype(BF16)

    for c in range(CHUNKS):
        cross(c)
    for c in range(CHUNKS):
        cross_copy(c).wait_recv()
    for side in range(2):
        for c in range(CHUNKS):
            for j in range(nz):
                r, a = cut(j)
                base = side * cols + c * ccols
                gw_ref[r, base + a.start:base + a.stop] = final[side, c, j].astype(F32)

    @pl.when(has_right)
    def _():
        for copy in to_right:
            copy.wait_send()
        for s in range(n_dp):
            halo_copy(s, 1).wait_send()

    @pl.when(has_left)
    def _():
        for copy in to_left:
            copy.wait_send()
        for s in range(n_dp):
            halo_copy(s, 0).wait_send()

    g_copy.wait_send()
    for k in range(n_dp - 1):
        w_copies[k].wait_send()
        w_forward(k).wait_send()
    for s in range(n_dp):
        ao_copy(s).wait_send()
    for c in range(CHUNKS):
        for k in range(n_dp - 1):
            part_copy(c, k).wait_send()
        for k in range(nz - 1):
            z_copy(c, k).wait_send()
            final_copy(c, k).wait_send()
        cross_copy(c).wait_send()


def per_device(queries, keys, values, lengths, out_weight, grad_out):
    n_tm = lax.axis_size("tm")
    n_dp = lax.axis_size("dp")
    rows, width = queries.shape[1:]
    shard = width // n_dp
    span = rows + 2 * WIN
    nz = n_tm // 2
    cols = width // 2
    ccols = cols // CHUNKS
    _, _, prow, pcol = piece_grid(nz, shard, ccols)
    inv_count = 1.0 / math.sqrt(n_dp * rows * n_tm)
    vmem = pl.BlockSpec(memory_space=pltpu.VMEM)
    hbm = pl.BlockSpec(memory_space=pl.ANY)
    dma = pltpu.SemaphoreType.DMA
    block = jax.ShapeDtypeStruct((rows, width), BF16)
    outs = pl.pallas_call(
        functools.partial(kernel, n_tm, n_dp, inv_count),
        out_shape=(block, block, block, block, jax.ShapeDtypeStruct((shard, width), F32)),
        in_specs=[pl.BlockSpec(memory_space=pltpu.SMEM), vmem, hbm, hbm, hbm, vmem],
        out_specs=(vmem,) * 5,
        scratch_shapes=[
            pltpu.VMEM((span, width), BF16),
            pltpu.VMEM((span, width), BF16),
            pltpu.VMEM((n_dp, shard, width), BF16),
            pltpu.VMEM((rows, width), BF16),
            pltpu.VMEM((2, rows, cols), BF16),
            pltpu.VMEM((2 * rows, cols), BF16),
            pltpu.VMEM((n_dp, 2 * rows, shard), BF16),
            pltpu.VMEM((rows, shard), BF16),
            pltpu.VMEM((H, rows, span), F32),
            pltpu.VMEM((2, rows, width), F32),
            pltpu.VMEM((n_dp, 2, 2, WIN, shard), BF16),
            pltpu.VMEM((n_dp, 2, 2, WIN, shard), BF16),
            pltpu.VMEM((CHUNKS, n_dp - 1, shard, ccols), BF16),
            pltpu.VMEM((CHUNKS, n_dp - 1, shard, ccols), BF16),
            pltpu.VMEM((CHUNKS, shard, ccols), F32),
            pltpu.VMEM((CHUNKS, nz, prow, pcol), F32),
            pltpu.VMEM((CHUNKS, nz, prow, pcol), BF16),
            pltpu.VMEM((CHUNKS, nz - 1, prow, pcol), BF16),
            pltpu.VMEM((2, CHUNKS, nz, prow, pcol), BF16),
            dma((3,)),
            dma((2, 2)), dma((2, 2)),
            dma((n_dp - 1,)), dma((n_dp - 1,)),
            dma((n_dp - 1,)), dma((n_dp - 1,)),
            dma(()), dma(()),
            dma((n_dp,)), dma((n_dp,)),
            dma((n_dp, 2)), dma((n_dp, 2)),
            dma((CHUNKS, n_dp - 1)), dma((CHUNKS, n_dp - 1)),
            dma((CHUNKS, nz - 1)), dma((CHUNKS, nz - 1)),
            dma((CHUNKS, nz - 1)), dma((CHUNKS, nz - 1)),
            dma((CHUNKS,)), dma((CHUNKS,)),
        ],
        compiler_params=pltpu.CompilerParams(
            collective_id=0, has_side_effects=True, vmem_limit_bytes=48 * 1024 * 1024
        ),
        cost_estimate=pl.CostEstimate(flops=4_000_000_000, bytes_accessed=8_000_000, transcendentals=1_000_000),
    )(lengths, queries[0], keys[0], values[0], out_weight, grad_out[0])
    attended, dq, dk, dv, gw = outs
    return (attended[None], dq[None], dk[None], dv[None], gw)


def solution(mesh):
    frames = P(("groups", "dp"), "tm", None)
    return jax.shard_map(
        per_device,
        mesh=mesh,
        in_specs=(frames, frames, frames, P(("groups", "dp")), P("dp", None), frames),
        out_specs=(frames, frames, frames, frames, P(("groups", "dp"), None)),
        check_vma=False,
    )
```

```python
import functools
import math

import jax
import jax.numpy as jnp
from jax import lax
from jax.experimental import pallas as pl
from jax.experimental.pallas import tpu as pltpu
from jax.sharding import PartitionSpec as P

H = 8
WIN = 128
CHUNKS = 2
PARTS = 4
NEG_FILL = -1000000000.0
F32 = jnp.float32
BF16 = jnp.bfloat16


def dot(a, b, over_a, over_b):
    return lax.dot_general(a, b, (((over_a,), (over_b,)), ((), ())), preferred_element_type=F32)


def piece_grid(nz, shard, cols):
    down = min(nz, shard // 16)
    across = nz // down
    return down, across, shard // down, cols // across


def kernel(
    n_tm, n_dp, inv_count,
    len_ref, q_hbm, k_hbm, v_hbm, w_hbm, g_hbm,
    att_ref, dq_ref, dk_ref, dv_ref, gw_ref,
    q_ref, g_ref, kext, vext, wfull, gm, gsplit, gg, ao, probs, mids, halo_out, halo_in,
    part_out, part_in, acc, z_own, z_out, z_in, final,
    own_sem, kv_send, kv_recv, w_send, w_recv, wf_send, wf_recv, g_send, g_recv,
    ao_send, ao_recv, h_send, h_recv, p_send, p_recv, z_send, z_recv,
    f_send, f_recv, x_send, x_recv,
):
    rows, width = q_hbm.shape
    shard = width // n_dp
    half = shard // 2
    head = width // H
    heads = shard // head
    nz = n_tm // 2
    cols = width // 2
    ccols = cols // CHUNKS
    scale = 1.0 / math.sqrt(head)
    down, across, prow, pcol = piece_grid(nz, shard, ccols)

    tm = lax.axis_index("tm")
    dp = lax.axis_index("dp")
    z = tm // 2
    core = tm % 2
    partner = tm + 1 - 2 * core
    right = lax.rem(tm + 1, n_tm)
    left = lax.rem(tm + n_tm - 1, n_tm)
    has_left = tm > 0
    has_right = tm < n_tm - 1

    def peer(k):
        return lax.rem(dp + k, n_dp)

    def z_peer(k):
        return lax.rem(z + k, nz)

    def remote(src, dst, send, recv, **where):
        return pltpu.make_async_remote_copy(
            src_ref=src, dst_ref=dst, send_sem=send, recv_sem=recv,
            device_id=where, device_id_type=pl.DeviceIdType.MESH,
        )

    own = [
        pltpu.make_async_copy(k_hbm, kext.at[pl.ds(WIN, rows)], own_sem.at[0]),
        pltpu.make_async_copy(v_hbm, vext.at[pl.ds(WIN, rows)], own_sem.at[1]),
        pltpu.make_async_copy(w_hbm, wfull.at[dp], own_sem.at[2]),
        pltpu.make_async_copy(q_hbm, q_ref, own_sem.at[3]),
        pltpu.make_async_copy(g_hbm, g_ref, own_sem.at[4]),
    ]
    for copy in own:
        copy.start()

    barrier = pltpu.get_barrier_semaphore()
    for t in (left, right):
        pl.semaphore_signal(barrier, inc=1, device_id={"tm": t}, device_id_type=pl.DeviceIdType.MESH)
    for k in range(1, n_dp):
        pl.semaphore_signal(barrier, inc=1, device_id={"dp": peer(k)}, device_id_type=pl.DeviceIdType.MESH)
    for k in range(1, nz):
        pl.semaphore_signal(
            barrier, inc=1, device_id={"tm": 2 * z_peer(k) + core}, device_id_type=pl.DeviceIdType.MESH
        )
    pl.semaphore_wait(barrier, 2 + (n_dp - 1) + (nz - 1))

    def turn(i):
        return lax.rem(dp + 1 + i, n_dp)

    def kv_copies(s, side):
        at = pl.ds(pl.multiple_of(s * shard, shard), shard)
        src, dst = ((rows - WIN, 0), (0, WIN + rows))[side]
        return [
            remote(
                hbm.at[pl.ds(src, WIN), at], ext.at[pl.ds(dst, WIN), at],
                kv_send.at[side, which, s], kv_recv.at[side, which, s], tm=(right, left)[side],
            )
            for which, (hbm, ext) in enumerate(((k_hbm, kext), (v_hbm, vext)))
        ]

    for i in range(n_dp):
        @pl.when(has_right)
        def _():
            for copy in kv_copies(turn(i), 0):
                copy.start()

        @pl.when(has_left)
        def _():
            for copy in kv_copies(turn(i), 1):
                copy.start()

    w_half = pl.ds(pl.multiple_of(core * half, half), half)
    w_copies = [
        remote(w_hbm.at[w_half], wfull.at[dp, w_half], w_send.at[k], w_recv.at[k], dp=peer(k + 1))
        for k in range(n_dp - 1)
    ]
    for copy in w_copies:
        copy.start()

    own[4].wait()
    length = len_ref[0]
    start = tm * rows
    row_pos = start + lax.broadcasted_iota(jnp.int32, (rows, 1), 0)
    valid = row_pos < length
    masked_grad = jnp.where(valid, g_ref[...].astype(F32), 0.0).astype(BF16)
    gm[...] = masked_grad
    gsplit[0] = masked_grad[:, :cols]
    gsplit[1] = masked_grad[:, cols:]
    g_copy = remote(gsplit.at[1 - core], gg.at[pl.ds(rows, rows)], g_send, g_recv, tm=partner)
    g_copy.start()
    gg[pl.ds(0, rows), :] = gsplit[core]

    @pl.when(jnp.logical_not(has_left))
    def _():
        kext[pl.ds(0, WIN), :] = jnp.zeros((WIN, width), BF16)
        vext[pl.ds(0, WIN), :] = jnp.zeros((WIN, width), BF16)
        halo_in[:, 1] = jnp.zeros((n_dp, 2, WIN, shard), BF16)

    @pl.when(jnp.logical_not(has_right))
    def _():
        kext[pl.ds(WIN + rows, WIN), :] = jnp.zeros((WIN, width), BF16)
        vext[pl.ds(WIN + rows, WIN), :] = jnp.zeros((WIN, width), BF16)
        halo_in[:, 0] = jnp.zeros((n_dp, 2, WIN, shard), BF16)

    for copy in own[:4]:
        copy.wait()

    span = rows + 2 * WIN
    q_pos = start + lax.broadcasted_iota(jnp.int32, (rows, span), 0)
    k_pos = start - WIN + lax.broadcasted_iota(jnp.int32, (rows, span), 1)
    allowed = (jnp.abs(q_pos - k_pos) <= WIN) & (k_pos >= 0) & (k_pos < length)
    bias = jnp.where(allowed, 0.0, NEG_FILL)
    live = jnp.where(valid, 1.0, 0.0)

    def ao_copy(s):
        return remote(
            ao.at[s, pl.ds(0, rows)], ao.at[s, pl.ds(rows, rows)], ao_send.at[s], ao_recv.at[s], tm=partner
        )

    def part_copy(c, k):
        return remote(
            part_out.at[c, k], part_in.at[c, k], p_send.at[c, k], p_recv.at[c, k], dp=peer(k + 1)
        )

    def send_part(k):
        s = peer(k + 1)
        ao_copy(s).wait_recv()
        for c in range(CHUNKS):
            part_out[c, k] = dot(ao[s], gg[:, c * ccols:(c + 1) * ccols], 0, 0).astype(BF16)
            part_copy(c, k).start()

    g_copy.wait_recv()

    @pl.loop(0, n_dp)
    def _(step):
        s = turn(step)

        @pl.when(has_left)
        def _():
            for copy in kv_copies(s, 0):
                copy.wait_recv()

        @pl.when(has_right)
        def _():
            for copy in kv_copies(s, 1):
                copy.wait_recv()

        at = pl.ds(pl.multiple_of(s * shard, shard), shard)
        q, k, v = q_ref[:, at], kext[:, at], vext[:, at]
        for i in range(heads):
            lanes = slice(i * head, (i + 1) * head)
            masked = dot(q[:, lanes], k[:, lanes], 1, 1) * scale + bias
            top = jnp.max(masked, axis=-1, keepdims=True)
            e = jnp.exp(masked - top)
            p = e * (live / jnp.sum(e, axis=-1, keepdims=True))
            probs[s * heads + i] = p
            ao[s, pl.ds(0, rows), lanes] = dot(p.astype(BF16), v[:, lanes], 1, 0).astype(BF16)
        ao_copy(s).start()

        @pl.when(step > 0)
        def _():
            send_part(step - 1)

    ao_copy(dp).wait_recv()
    for c in range(CHUNKS):
        acc[c] = dot(ao[dp], gg[:, c * ccols:(c + 1) * ccols], 0, 0)

    def w_copy(k):
        return remote(w_hbm.at[w_half], wfull.at[dp, w_half], w_send.at[k], w_recv.at[k], dp=peer(k + 1))

    def w_forward(k):
        src = lax.rem(dp + n_dp - 1 - k, n_dp)
        return remote(
            wfull.at[src, w_half], wfull.at[src, w_half], wf_send.at[k], wf_recv.at[k], tm=partner
        )

    def halo_copy(s, side):
        return remote(
            halo_out.at[s, side], halo_in.at[s, side], h_send.at[s, side], h_recv.at[s, side],
            tm=(left, right)[side],
        )

    @pl.loop(0, n_dp)
    def _(step):
        s = lax.rem(dp + n_dp - step, n_dp)

        @pl.when(step < n_dp - 1)
        def _():
            w_copy(step).wait_recv()
            w_forward(step).start()

        @pl.when(step > 0)
        def _():
            w_forward(step - 1).wait_recv()

        at = pl.ds(pl.multiple_of(s * shard, shard), shard)
        q, k, v = q_ref[:, at], kext[:, at], vext[:, at]
        grad_attn = dot(gm[...], wfull[s], 1, 1).astype(BF16)
        for i in range(heads):
            lanes = slice(i * head, (i + 1) * head)
            p = probs[s * heads + i]
            grad_probs = dot(grad_attn[:, lanes], v[:, lanes], 1, 1)
            delta = jnp.sum(p * grad_probs, axis=-1, keepdims=True)
            grad_scores = (p * (grad_probs - delta) * scale).astype(BF16)
            hd = pl.ds(pl.multiple_of(s * shard + i * head, head), head)
            dq_ref[:, hd] = dot(grad_scores, k[:, lanes], 1, 0).astype(BF16)
            terms = (
                dot(grad_scores, q[:, lanes], 0, 0),
                dot(p.astype(BF16), grad_attn[:, lanes], 0, 0),
            )
            for which, term in enumerate(terms):
                halo_out[s, 0, which, :, lanes] = term[:WIN].astype(BF16)
                halo_out[s, 1, which, :, lanes] = term[WIN + rows:].astype(BF16)
                mids[which, :, hd] = term[WIN:WIN + rows]

        @pl.when(has_left)
        def _():
            halo_copy(s, 0).start()

        @pl.when(has_right)
        def _():
            halo_copy(s, 1).start()

    def z_copy(c, k):
        return remote(
            z_out.at[c, z_peer(k + 1)], z_in.at[c, k], z_send.at[c, k], z_recv.at[c, k],
            tm=2 * z_peer(k + 1) + core,
        )

    def final_copy(c, k):
        return remote(
            final.at[core, c, z], final.at[core, c, z], f_send.at[c, k], f_recv.at[c, k],
            tm=2 * z_peer(k + 1) + core,
        )

    def cross_copy(c):
        return remote(final.at[core, c], final.at[core, c], x_send.at[c], x_recv.at[c], tm=partner)

    def cut(j):
        r, a = (j // across) * prow, (j % across) * pcol
        return slice(r, r + prow), slice(a, a + pcol)

    def scatter(c):
        total = acc[c]
        for k in range(n_dp - 1):
            part_copy(c, k).wait_recv()
            total = total + part_in[c, k].astype(F32)
        for j in range(nz):
            r, a = cut(j)
            z_own[c, j] = total[r, a]
            z_out[c, j] = total[r, a].astype(BF16)
        for k in range(nz - 1):
            z_copy(c, k).start()

    def gather(c):
        total = z_own[c, z]
        for k in range(nz - 1):
            z_copy(c, k).wait_recv()
            total = total + z_in[c, k].astype(F32)
        final[core, c, z] = (total * inv_count).astype(BF16)
        for k in range(nz - 1):
            final_copy(c, k).start()

    def cross(c):
        for k in range(nz - 1):
            final_copy(c, k).wait_recv()
        cross_copy(c).start()

    attended = dot(ao[0, pl.ds(0, rows)], wfull[0], 1, 0)
    for s in range(1, n_dp):
        attended += dot(ao[s, pl.ds(0, rows)], wfull[s], 1, 0)
    att_ref[...] = jnp.where(valid, attended, 0.0).astype(BF16)

    for c in range(CHUNKS):
        scatter(c)
    for c in range(CHUNKS):
        gather(c)

    @pl.when(has_right)
    def _():
        for s in range(n_dp):
            halo_copy(s, 0).wait_recv()

    @pl.when(has_left)
    def _():
        for s in range(n_dp):
            halo_copy(s, 1).wait_recv()

    for which, out in enumerate((dk_ref, dv_ref)):
        for s in range(n_dp):
            lanes = slice(s * shard, (s + 1) * shard)
            out[0:WIN, lanes] = (
                mids[which, 0:WIN, lanes] + halo_in[s, 1, which].astype(F32)
            ).astype(BF16)
            if rows > 2 * WIN:
                out[WIN:rows - WIN, lanes] = mids[which, WIN:rows - WIN, lanes].astype(BF16)
            out[rows - WIN:rows, lanes] = (
                mids[which, rows - WIN:rows, lanes] + halo_in[s, 0, which].astype(F32)
            ).astype(BF16)

    for c in range(CHUNKS):
        cross(c)
    for c in range(CHUNKS):
        cross_copy(c).wait_recv()
    for side in range(2):
        for c in range(CHUNKS):
            for j in range(nz):
                r, a = cut(j)
                base = side * cols + c * ccols
                gw_ref[r, base + a.start:base + a.stop] = final[side, c, j].astype(F32)

    @pl.when(has_right)
    def _():
        for s in range(n_dp):
            for copy in kv_copies(s, 0):
                copy.wait_send()
            halo_copy(s, 1).wait_send()

    @pl.when(has_left)
    def _():
        for s in range(n_dp):
            for copy in kv_copies(s, 1):
                copy.wait_send()
            halo_copy(s, 0).wait_send()

    g_copy.wait_send()
    for k in range(n_dp - 1):
        w_copies[k].wait_send()
        w_forward(k).wait_send()
    for s in range(n_dp):
        ao_copy(s).wait_send()
    for c in range(CHUNKS):
        for k in range(n_dp - 1):
            part_copy(c, k).wait_send()
        for k in range(nz - 1):
            z_copy(c, k).wait_send()
            final_copy(c, k).wait_send()
        cross_copy(c).wait_send()


def hand_over_kernel(count, *refs):
    srcs, dsts, held = refs[:count], refs[count:2 * count], refs[2 * count:3 * count]
    sem_in, sem_out = refs[3 * count:]
    loads, stores = [], []
    for i in range(count):
        part = srcs[i].shape[0] // PARTS
        for j in range(PARTS):
            at = pl.ds(j * part, part)
            loads.append(pltpu.make_async_copy(srcs[i].at[at], held[i].at[at], sem_in.at[i, j]))
            stores.append(pltpu.make_async_copy(held[i].at[at], dsts[i].at[at], sem_out.at[i, j]))
    for load in loads:
        load.start()
    for load, store in zip(loads, stores):
        load.wait()
        store.start()
    for store in stores:
        store.wait()


def hand_over(arrays):
    hbm = pl.BlockSpec(memory_space=pl.ANY)
    return pl.pallas_call(
        functools.partial(hand_over_kernel, len(arrays)),
        out_shape=tuple(jax.ShapeDtypeStruct(a.shape, a.dtype) for a in arrays),
        in_specs=[hbm] * len(arrays),
        out_specs=(hbm,) * len(arrays),
        scratch_shapes=[pltpu.VMEM(a.shape, a.dtype) for a in arrays]
        + [pltpu.SemaphoreType.DMA((len(arrays), PARTS))] * 2,
        compiler_params=pltpu.CompilerParams(vmem_limit_bytes=60 * 1024 * 1024),
    )(*arrays)


def per_device(queries, keys, values, lengths, out_weight, grad_out):
    n_tm = lax.axis_size("tm")
    n_dp = lax.axis_size("dp")
    rows, width = queries.shape[1:]
    shard = width // n_dp
    span = rows + 2 * WIN
    nz = n_tm // 2
    cols = width // 2
    ccols = cols // CHUNKS
    _, _, prow, pcol = piece_grid(nz, shard, ccols)
    inv_count = 1.0 / math.sqrt(n_dp * rows * n_tm)
    vmem = pl.BlockSpec(memory_space=pltpu.VMEM)
    hbm = pl.BlockSpec(memory_space=pl.ANY)
    dma = pltpu.SemaphoreType.DMA
    block = jax.ShapeDtypeStruct((rows, width), BF16)
    outs = pl.pallas_call(
        functools.partial(kernel, n_tm, n_dp, inv_count),
        out_shape=(block, block, block, block, jax.ShapeDtypeStruct((shard, width), F32)),
        in_specs=[pl.BlockSpec(memory_space=pltpu.SMEM), hbm, hbm, hbm, hbm, hbm],
        out_specs=(vmem,) * 5,
        scratch_shapes=[
            pltpu.VMEM((rows, width), BF16),
            pltpu.VMEM((rows, width), BF16),
            pltpu.VMEM((span, width), BF16),
            pltpu.VMEM((span, width), BF16),
            pltpu.VMEM((n_dp, shard, width), BF16),
            pltpu.VMEM((rows, width), BF16),
            pltpu.VMEM((2, rows, cols), BF16),
            pltpu.VMEM((2 * rows, cols), BF16),
            pltpu.VMEM((n_dp, 2 * rows, shard), BF16),
            pltpu.VMEM((H, rows, span), F32),
            pltpu.VMEM((2, rows, width), F32),
            pltpu.VMEM((n_dp, 2, 2, WIN, shard), BF16),
            pltpu.VMEM((n_dp, 2, 2, WIN, shard), BF16),
            pltpu.VMEM((CHUNKS, n_dp - 1, shard, ccols), BF16),
            pltpu.VMEM((CHUNKS, n_dp - 1, shard, ccols), BF16),
            pltpu.VMEM((CHUNKS, shard, ccols), F32),
            pltpu.VMEM((CHUNKS, nz, prow, pcol), F32),
            pltpu.VMEM((CHUNKS, nz, prow, pcol), BF16),
            pltpu.VMEM((CHUNKS, nz - 1, prow, pcol), BF16),
            pltpu.VMEM((2, CHUNKS, nz, prow, pcol), BF16),
            dma((5,)),
            dma((2, 2, n_dp)), dma((2, 2, n_dp)),
            dma((n_dp - 1,)), dma((n_dp - 1,)),
            dma((n_dp - 1,)), dma((n_dp - 1,)),
            dma(()), dma(()),
            dma((n_dp,)), dma((n_dp,)),
            dma((n_dp, 2)), dma((n_dp, 2)),
            dma((CHUNKS, n_dp - 1)), dma((CHUNKS, n_dp - 1)),
            dma((CHUNKS, nz - 1)), dma((CHUNKS, nz - 1)),
            dma((CHUNKS, nz - 1)), dma((CHUNKS, nz - 1)),
            dma((CHUNKS,)), dma((CHUNKS,)),
        ],
        compiler_params=pltpu.CompilerParams(
            collective_id=0, has_side_effects=True, vmem_limit_bytes=60 * 1024 * 1024
        ),
        cost_estimate=pl.CostEstimate(flops=4_000_000_000, bytes_accessed=8_000_000, transcendentals=1_000_000),
    )(lengths, queries[0], keys[0], values[0], out_weight, grad_out[0])
    attended, dq, dk, dv, gw = hand_over(outs)
    return (attended[None], dq[None], dk[None], dv[None], gw)


def solution(mesh):
    frames = P(("groups", "dp"), "tm", None)
    return jax.shard_map(
        per_device,
        mesh=mesh,
        in_specs=(frames, frames, frames, P(("groups", "dp")), P("dp", None), frames),
        out_specs=(frames, frames, frames, frames, P(("groups", "dp"), None)),
        check_vma=False,
    )
```

```python
import functools
import math

import jax
import jax.numpy as jnp
from jax import lax
from jax.experimental import pallas as pl
from jax.experimental.pallas import tpu as pltpu
from jax.sharding import PartitionSpec as P

H = 8
WIN = 128
CHUNKS = 2
PARTS = 2
NEG_FILL = -1000000000.0
F32 = jnp.float32
BF16 = jnp.bfloat16


def dot(a, b, over_a, over_b):
    return lax.dot_general(a, b, (((over_a,), (over_b,)), ((), ())), preferred_element_type=F32)


def piece_grid(nz, shard, cols):
    down = min(nz, shard // 16)
    across = nz // down
    return down, across, shard // down, cols // across


def kernel(
    n_tm, n_dp, inv_count,
    len_ref, q_hbm, k_hbm, v_hbm, w_hbm, g_hbm,
    att_ref, dq_ref, dk_ref, dv_ref, gw_ref,
    q_ref, g_ref, kext, vext, wfull, gm, gsplit, gg, ao, probs, mids, halo_out, halo_in,
    part_out, part_in, acc, z_own, z_out, z_in, final,
    own_sem, kv_send, kv_recv, w_send, w_recv, wf_send, wf_recv, g_send, g_recv,
    ao_send, ao_recv, h_send, h_recv, p_send, p_recv, z_send, z_recv,
    f_send, f_recv, x_send, x_recv,
):
    rows, width = q_hbm.shape
    shard = width // n_dp
    half = shard // 2
    head = width // H
    heads = shard // head
    nz = n_tm // 2
    cols = width // 2
    ccols = cols // CHUNKS
    scale = 1.0 / math.sqrt(head)
    down, across, prow, pcol = piece_grid(nz, shard, ccols)

    tm = lax.axis_index("tm")
    dp = lax.axis_index("dp")
    z = tm // 2
    core = tm % 2
    partner = tm + 1 - 2 * core
    right = lax.rem(tm + 1, n_tm)
    left = lax.rem(tm + n_tm - 1, n_tm)
    has_left = tm > 0
    has_right = tm < n_tm - 1

    def peer(k):
        return lax.rem(dp + k, n_dp)

    def z_peer(k):
        return lax.rem(z + k, nz)

    def remote(src, dst, send, recv, **where):
        return pltpu.make_async_remote_copy(
            src_ref=src, dst_ref=dst, send_sem=send, recv_sem=recv,
            device_id=where, device_id_type=pl.DeviceIdType.MESH,
        )

    own = [
        pltpu.make_async_copy(k_hbm, kext.at[pl.ds(WIN, rows)], own_sem.at[0]),
        pltpu.make_async_copy(v_hbm, vext.at[pl.ds(WIN, rows)], own_sem.at[1]),
        pltpu.make_async_copy(w_hbm, wfull.at[dp], own_sem.at[2]),
        pltpu.make_async_copy(q_hbm, q_ref, own_sem.at[3]),
        pltpu.make_async_copy(g_hbm, g_ref, own_sem.at[4]),
    ]
    for copy in own:
        copy.start()

    barrier = pltpu.get_barrier_semaphore()
    for t in (left, right):
        pl.semaphore_signal(barrier, inc=1, device_id={"tm": t}, device_id_type=pl.DeviceIdType.MESH)
    for k in range(1, n_dp):
        pl.semaphore_signal(barrier, inc=1, device_id={"dp": peer(k)}, device_id_type=pl.DeviceIdType.MESH)
    for k in range(1, nz):
        pl.semaphore_signal(
            barrier, inc=1, device_id={"tm": 2 * z_peer(k) + core}, device_id_type=pl.DeviceIdType.MESH
        )
    pl.semaphore_wait(barrier, 2 + (n_dp - 1) + (nz - 1))

    def turn(i):
        return lax.rem(dp + 1 + i, n_dp)

    def kv_copies(s, side):
        at = pl.ds(pl.multiple_of(s * shard, shard), shard)
        src, dst = ((rows - WIN, 0), (0, WIN + rows))[side]
        return [
            remote(
                hbm.at[pl.ds(src, WIN), at], ext.at[pl.ds(dst, WIN), at],
                kv_send.at[side, which, s], kv_recv.at[side, which, s], tm=(right, left)[side],
            )
            for which, (hbm, ext) in enumerate(((k_hbm, kext), (v_hbm, vext)))
        ]

    for i in range(n_dp):
        @pl.when(has_right)
        def _():
            for copy in kv_copies(turn(i), 0):
                copy.start()

        @pl.when(has_left)
        def _():
            for copy in kv_copies(turn(i), 1):
                copy.start()

    w_half = pl.ds(pl.multiple_of(core * half, half), half)
    w_copies = [
        remote(w_hbm.at[w_half], wfull.at[dp, w_half], w_send.at[k], w_recv.at[k], dp=peer(k + 1))
        for k in range(n_dp - 1)
    ]
    for copy in w_copies:
        copy.start()

    own[4].wait()
    length = len_ref[0]
    start = tm * rows
    row_pos = start + lax.broadcasted_iota(jnp.int32, (rows, 1), 0)
    valid = row_pos < length
    masked_grad = jnp.where(valid, g_ref[...].astype(F32), 0.0).astype(BF16)
    gm[...] = masked_grad
    gsplit[0] = masked_grad[:, :cols]
    gsplit[1] = masked_grad[:, cols:]
    g_copy = remote(gsplit.at[1 - core], gg.at[pl.ds(rows, rows)], g_send, g_recv, tm=partner)
    g_copy.start()
    gg[pl.ds(0, rows), :] = gsplit[core]

    @pl.when(jnp.logical_not(has_left))
    def _():
        kext[pl.ds(0, WIN), :] = jnp.zeros((WIN, width), BF16)
        vext[pl.ds(0, WIN), :] = jnp.zeros((WIN, width), BF16)
        halo_in[:, 1] = jnp.zeros((n_dp, 2, WIN, shard), BF16)

    @pl.when(jnp.logical_not(has_right))
    def _():
        kext[pl.ds(WIN + rows, WIN), :] = jnp.zeros((WIN, width), BF16)
        vext[pl.ds(WIN + rows, WIN), :] = jnp.zeros((WIN, width), BF16)
        halo_in[:, 0] = jnp.zeros((n_dp, 2, WIN, shard), BF16)

    for copy in own[:4]:
        copy.wait()

    span = rows + 2 * WIN
    q_pos = start + lax.broadcasted_iota(jnp.int32, (rows, span), 0)
    k_pos = start - WIN + lax.broadcasted_iota(jnp.int32, (rows, span), 1)
    allowed = (jnp.abs(q_pos - k_pos) <= WIN) & (k_pos >= 0) & (k_pos < length)
    bias = jnp.where(allowed, 0.0, NEG_FILL)
    live = jnp.where(valid, 1.0, 0.0)

    def ao_copy(s):
        return remote(
            ao.at[s, pl.ds(0, rows)], ao.at[s, pl.ds(rows, rows)], ao_send.at[s], ao_recv.at[s], tm=partner
        )

    def part_copy(c, k):
        return remote(
            part_out.at[c, k], part_in.at[c, k], p_send.at[c, k], p_recv.at[c, k], dp=peer(k + 1)
        )

    def send_part(k):
        s = peer(k + 1)
        ao_copy(s).wait_recv()
        for c in range(CHUNKS):
            part_out[c, k] = dot(ao[s], gg[:, c * ccols:(c + 1) * ccols], 0, 0).astype(BF16)
            part_copy(c, k).start()

    g_copy.wait_recv()

    @pl.loop(0, n_dp)
    def _(step):
        s = turn(step)

        @pl.when(has_left)
        def _():
            for copy in kv_copies(s, 0):
                copy.wait_recv()

        @pl.when(has_right)
        def _():
            for copy in kv_copies(s, 1):
                copy.wait_recv()

        at = pl.ds(pl.multiple_of(s * shard, shard), shard)
        q, k, v = q_ref[:, at], kext[:, at], vext[:, at]
        for i in range(heads):
            lanes = slice(i * head, (i + 1) * head)
            masked = dot(q[:, lanes], k[:, lanes], 1, 1) * scale + bias
            top = jnp.max(masked, axis=-1, keepdims=True)
            e = jnp.exp(masked - top)
            p = e * (live / jnp.sum(e, axis=-1, keepdims=True))
            probs[s * heads + i] = p
            ao[s, pl.ds(0, rows), lanes] = dot(p.astype(BF16), v[:, lanes], 1, 0).astype(BF16)
        ao_copy(s).start()

        @pl.when(step > 0)
        def _():
            send_part(step - 1)

    ao_copy(dp).wait_recv()
    for c in range(CHUNKS):
        acc[c] = dot(ao[dp], gg[:, c * ccols:(c + 1) * ccols], 0, 0)

    def w_copy(k):
        return remote(w_hbm.at[w_half], wfull.at[dp, w_half], w_send.at[k], w_recv.at[k], dp=peer(k + 1))

    def w_forward(k):
        src = lax.rem(dp + n_dp - 1 - k, n_dp)
        return remote(
            wfull.at[src, w_half], wfull.at[src, w_half], wf_send.at[k], wf_recv.at[k], tm=partner
        )

    def halo_copy(s, side):
        return remote(
            halo_out.at[s, side], halo_in.at[s, side], h_send.at[s, side], h_recv.at[s, side],
            tm=(left, right)[side],
        )

    @pl.loop(0, n_dp)
    def _(step):
        s = lax.rem(dp + n_dp - step, n_dp)

        @pl.when(step < n_dp - 1)
        def _():
            w_copy(step).wait_recv()
            w_forward(step).start()

        @pl.when(step > 0)
        def _():
            w_forward(step - 1).wait_recv()

        at = pl.ds(pl.multiple_of(s * shard, shard), shard)
        q, k, v = q_ref[:, at], kext[:, at], vext[:, at]
        grad_attn = dot(gm[...], wfull[s], 1, 1).astype(BF16)
        for i in range(heads):
            lanes = slice(i * head, (i + 1) * head)
            p = probs[s * heads + i]
            grad_probs = dot(grad_attn[:, lanes], v[:, lanes], 1, 1)
            delta = jnp.sum(p * grad_probs, axis=-1, keepdims=True)
            grad_scores = (p * (grad_probs - delta) * scale).astype(BF16)
            hd = pl.ds(pl.multiple_of(s * shard + i * head, head), head)
            dq_ref[:, hd] = dot(grad_scores, k[:, lanes], 1, 0).astype(BF16)
            terms = (
                dot(grad_scores, q[:, lanes], 0, 0),
                dot(p.astype(BF16), grad_attn[:, lanes], 0, 0),
            )
            for which, term in enumerate(terms):
                halo_out[s, 0, which, :, lanes] = term[:WIN].astype(BF16)
                halo_out[s, 1, which, :, lanes] = term[WIN + rows:].astype(BF16)
                mids[which, :, hd] = term[WIN:WIN + rows]

        @pl.when(has_left)
        def _():
            halo_copy(s, 0).start()

        @pl.when(has_right)
        def _():
            halo_copy(s, 1).start()

    def z_copy(c, k):
        return remote(
            z_out.at[c, z_peer(k + 1)], z_in.at[c, k], z_send.at[c, k], z_recv.at[c, k],
            tm=2 * z_peer(k + 1) + core,
        )

    def final_copy(c, k):
        return remote(
            final.at[core, c, z], final.at[core, c, z], f_send.at[c, k], f_recv.at[c, k],
            tm=2 * z_peer(k + 1) + core,
        )

    def cross_copy(c):
        return remote(final.at[core, c], final.at[core, c], x_send.at[c], x_recv.at[c], tm=partner)

    def cut(j):
        r, a = (j // across) * prow, (j % across) * pcol
        return slice(r, r + prow), slice(a, a + pcol)

    def scatter(c):
        total = acc[c]
        for k in range(n_dp - 1):
            part_copy(c, k).wait_recv()
            total = total + part_in[c, k].astype(F32)
        for j in range(nz):
            r, a = cut(j)
            z_own[c, j] = total[r, a]
            z_out[c, j] = total[r, a].astype(BF16)
        for k in range(nz - 1):
            z_copy(c, k).start()

    def gather(c):
        total = z_own[c, z]
        for k in range(nz - 1):
            z_copy(c, k).wait_recv()
            total = total + z_in[c, k].astype(F32)
        final[core, c, z] = (total * inv_count).astype(BF16)
        for k in range(nz - 1):
            final_copy(c, k).start()

    def cross(c):
        for k in range(nz - 1):
            final_copy(c, k).wait_recv()
        cross_copy(c).start()

    for c in range(CHUNKS):
        scatter(c)

    attended = dot(ao[0, pl.ds(0, rows)], wfull[0], 1, 0)
    for s in range(1, n_dp):
        attended += dot(ao[s, pl.ds(0, rows)], wfull[s], 1, 0)
    att_ref[...] = jnp.where(valid, attended, 0.0).astype(BF16)

    for c in range(CHUNKS):
        gather(c)

    @pl.when(has_right)
    def _():
        for s in range(n_dp):
            halo_copy(s, 0).wait_recv()

    @pl.when(has_left)
    def _():
        for s in range(n_dp):
            halo_copy(s, 1).wait_recv()

    for which, out in enumerate((dk_ref, dv_ref)):
        for s in range(n_dp):
            lanes = slice(s * shard, (s + 1) * shard)
            out[0:WIN, lanes] = (
                mids[which, 0:WIN, lanes] + halo_in[s, 1, which].astype(F32)
            ).astype(BF16)
            if rows > 2 * WIN:
                out[WIN:rows - WIN, lanes] = mids[which, WIN:rows - WIN, lanes].astype(BF16)
            out[rows - WIN:rows, lanes] = (
                mids[which, rows - WIN:rows, lanes] + halo_in[s, 0, which].astype(F32)
            ).astype(BF16)

    for c in range(CHUNKS):
        cross(c)
    for c in range(CHUNKS):
        cross_copy(c).wait_recv()
    for side in range(2):
        for c in range(CHUNKS):
            for j in range(nz):
                r, a = cut(j)
                base = side * cols + c * ccols
                gw_ref[r, base + a.start:base + a.stop] = final[side, c, j]

    @pl.when(has_right)
    def _():
        for s in range(n_dp):
            for copy in kv_copies(s, 0):
                copy.wait_send()
            halo_copy(s, 1).wait_send()

    @pl.when(has_left)
    def _():
        for s in range(n_dp):
            for copy in kv_copies(s, 1):
                copy.wait_send()
            halo_copy(s, 0).wait_send()

    g_copy.wait_send()
    for k in range(n_dp - 1):
        w_copies[k].wait_send()
        w_forward(k).wait_send()
    for s in range(n_dp):
        ao_copy(s).wait_send()
    for c in range(CHUNKS):
        for k in range(n_dp - 1):
            part_copy(c, k).wait_send()
        for k in range(nz - 1):
            z_copy(c, k).wait_send()
            final_copy(c, k).wait_send()
        cross_copy(c).wait_send()


def hand_over_kernel(count, *refs):
    srcs, dsts, held = refs[:count], refs[count:2 * count], refs[2 * count:3 * count]
    wide, sem_in, sem_out = refs[3 * count:]
    loads, stores = [], []
    for i in range(count):
        part = srcs[i].shape[0] // PARTS
        for j in range(PARTS):
            at = pl.ds(j * part, part)
            loads.append(pltpu.make_async_copy(srcs[i].at[at], held[i].at[at], sem_in.at[i, j]))
            ready = wide if i == count - 1 else held[i]
            stores.append(pltpu.make_async_copy(ready.at[at], dsts[i].at[at], sem_out.at[i, j]))
    for load in loads:
        load.start()
    for n, (load, store) in enumerate(zip(loads, stores)):
        load.wait()
        if n >= (count - 1) * PARTS:
            at = pl.ds((n - (count - 1) * PARTS) * part, part)
            wide[at, :] = held[-1][at, :].astype(F32)
        store.start()
    for store in stores:
        store.wait()


def hand_over(arrays):
    hbm = pl.BlockSpec(memory_space=pl.ANY)
    return pl.pallas_call(
        functools.partial(hand_over_kernel, len(arrays)),
        out_shape=tuple(jax.ShapeDtypeStruct(a.shape, a.dtype) for a in arrays[:-1])
        + (jax.ShapeDtypeStruct(arrays[-1].shape, F32),),
        in_specs=[hbm] * len(arrays),
        out_specs=(hbm,) * len(arrays),
        scratch_shapes=[pltpu.VMEM(a.shape, a.dtype) for a in arrays]
        + [pltpu.VMEM(arrays[-1].shape, F32)]
        + [pltpu.SemaphoreType.DMA((len(arrays), PARTS))] * 2,
        compiler_params=pltpu.CompilerParams(vmem_limit_bytes=60 * 1024 * 1024),
    )(*arrays)


def per_device(queries, keys, values, lengths, out_weight, grad_out):
    n_tm = lax.axis_size("tm")
    n_dp = lax.axis_size("dp")
    rows, width = queries.shape[1:]
    shard = width // n_dp
    span = rows + 2 * WIN
    nz = n_tm // 2
    cols = width // 2
    ccols = cols // CHUNKS
    _, _, prow, pcol = piece_grid(nz, shard, ccols)
    inv_count = 1.0 / math.sqrt(n_dp * rows * n_tm)
    vmem = pl.BlockSpec(memory_space=pltpu.VMEM)
    hbm = pl.BlockSpec(memory_space=pl.ANY)
    dma = pltpu.SemaphoreType.DMA
    block = jax.ShapeDtypeStruct((rows, width), BF16)
    outs = pl.pallas_call(
        functools.partial(kernel, n_tm, n_dp, inv_count),
        out_shape=(block, block, block, block, jax.ShapeDtypeStruct((shard, width), BF16)),
        in_specs=[pl.BlockSpec(memory_space=pltpu.SMEM), hbm, hbm, hbm, hbm, hbm],
        out_specs=(vmem,) * 5,
        scratch_shapes=[
            pltpu.VMEM((rows, width), BF16),
            pltpu.VMEM((rows, width), BF16),
            pltpu.VMEM((span, width), BF16),
            pltpu.VMEM((span, width), BF16),
            pltpu.VMEM((n_dp, shard, width), BF16),
            pltpu.VMEM((rows, width), BF16),
            pltpu.VMEM((2, rows, cols), BF16),
            pltpu.VMEM((2 * rows, cols), BF16),
            pltpu.VMEM((n_dp, 2 * rows, shard), BF16),
            pltpu.VMEM((H, rows, span), F32),
            pltpu.VMEM((2, rows, width), F32),
            pltpu.VMEM((n_dp, 2, 2, WIN, shard), BF16),
            pltpu.VMEM((n_dp, 2, 2, WIN, shard), BF16),
            pltpu.VMEM((CHUNKS, n_dp - 1, shard, ccols), BF16),
            pltpu.VMEM((CHUNKS, n_dp - 1, shard, ccols), BF16),
            pltpu.VMEM((CHUNKS, shard, ccols), F32),
            pltpu.VMEM((CHUNKS, nz, prow, pcol), F32),
            pltpu.VMEM((CHUNKS, nz, prow, pcol), BF16),
            pltpu.VMEM((CHUNKS, nz - 1, prow, pcol), BF16),
            pltpu.VMEM((2, CHUNKS, nz, prow, pcol), BF16),
            dma((5,)),
            dma((2, 2, n_dp)), dma((2, 2, n_dp)),
            dma((n_dp - 1,)), dma((n_dp - 1,)),
            dma((n_dp - 1,)), dma((n_dp - 1,)),
            dma(()), dma(()),
            dma((n_dp,)), dma((n_dp,)),
            dma((n_dp, 2)), dma((n_dp, 2)),
            dma((CHUNKS, n_dp - 1)), dma((CHUNKS, n_dp - 1)),
            dma((CHUNKS, nz - 1)), dma((CHUNKS, nz - 1)),
            dma((CHUNKS, nz - 1)), dma((CHUNKS, nz - 1)),
            dma((CHUNKS,)), dma((CHUNKS,)),
        ],
        compiler_params=pltpu.CompilerParams(
            collective_id=0, has_side_effects=True, vmem_limit_bytes=60 * 1024 * 1024
        ),
        cost_estimate=pl.CostEstimate(flops=4_000_000_000, bytes_accessed=8_000_000, transcendentals=1_000_000),
    )(lengths, queries[0], keys[0], values[0], out_weight, grad_out[0])
    attended, dq, dk, dv, gw = hand_over(outs)
    return (attended[None], dq[None], dk[None], dv[None], gw)


def solution(mesh):
    frames = P(("groups", "dp"), "tm", None)
    return jax.shard_map(
        per_device,
        mesh=mesh,
        in_specs=(frames, frames, frames, P(("groups", "dp")), P("dp", None), frames),
        out_specs=(frames, frames, frames, frames, P(("groups", "dp"), None)),
        check_vma=False,
    )
```

```python
import functools
import math

import jax
import jax.numpy as jnp
from jax import lax
from jax.experimental import pallas as pl
from jax.experimental.pallas import tpu as pltpu
from jax.sharding import PartitionSpec as P

H = 8
WIN = 128
CHUNKS = 2
PARTS = 2
NEG_FILL = -1000000000.0
F32 = jnp.float32
BF16 = jnp.bfloat16


def dot(a, b, over_a, over_b):
    return lax.dot_general(a, b, (((over_a,), (over_b,)), ((), ())), preferred_element_type=F32)


def piece_grid(nz, shard, cols):
    down = min(nz, shard // 16)
    across = nz // down
    return down, across, shard // down, cols // across


def kernel(
    n_tm, n_dp, inv_count,
    len_ref, q_hbm, k_hbm, v_hbm, w_hbm, g_hbm,
    att_ref, dq_ref, dk_ref, dv_ref, gw_ref,
    q_ref, g_ref, kext, vext, wfull, gm, gsplit, gg, ao, probs, mids, halo_out, halo_in,
    part_out, part_in, acc, z_own, z_out, z_in, final,
    own_sem, kv_send, kv_recv, w_send, w_recv, wf_send, wf_recv, g_send, g_recv,
    ao_send, ao_recv, h_send, h_recv, p_send, p_recv, z_send, z_recv,
    f_send, f_recv, x_send, x_recv,
):
    rows, width = q_hbm.shape
    shard = width // n_dp
    half = shard // 2
    head = width // H
    heads = shard // head
    nz = n_tm // 2
    cols = width // 2
    ccols = cols // CHUNKS
    scale = 1.0 / math.sqrt(head)
    down, across, prow, pcol = piece_grid(nz, shard, ccols)

    tm = lax.axis_index("tm")
    dp = lax.axis_index("dp")
    z = tm // 2
    core = tm % 2
    partner = tm + 1 - 2 * core
    right = lax.rem(tm + 1, n_tm)
    left = lax.rem(tm + n_tm - 1, n_tm)
    has_left = tm > 0
    has_right = tm < n_tm - 1

    def peer(k):
        return lax.rem(dp + k, n_dp)

    def z_peer(k):
        return lax.rem(z + k, nz)

    def remote(src, dst, send, recv, **where):
        return pltpu.make_async_remote_copy(
            src_ref=src, dst_ref=dst, send_sem=send, recv_sem=recv,
            device_id=where, device_id_type=pl.DeviceIdType.MESH,
        )

    own = [
        pltpu.make_async_copy(k_hbm, kext.at[pl.ds(WIN, rows)], own_sem.at[0]),
        pltpu.make_async_copy(v_hbm, vext.at[pl.ds(WIN, rows)], own_sem.at[1]),
        pltpu.make_async_copy(w_hbm, wfull.at[dp], own_sem.at[2]),
        pltpu.make_async_copy(q_hbm, q_ref, own_sem.at[3]),
        pltpu.make_async_copy(g_hbm, g_ref, own_sem.at[4]),
    ]
    for copy in own:
        copy.start()

    barrier = pltpu.get_barrier_semaphore()
    for t in (left, right):
        pl.semaphore_signal(barrier, inc=1, device_id={"tm": t}, device_id_type=pl.DeviceIdType.MESH)
    for k in range(1, n_dp):
        pl.semaphore_signal(barrier, inc=1, device_id={"dp": peer(k)}, device_id_type=pl.DeviceIdType.MESH)
    for k in range(1, nz):
        pl.semaphore_signal(
            barrier, inc=1, device_id={"tm": 2 * z_peer(k) + core}, device_id_type=pl.DeviceIdType.MESH
        )
    pl.semaphore_wait(barrier, 2 + (n_dp - 1) + (nz - 1))

    def turn(i):
        return lax.rem(dp + 1 + i, n_dp)

    def kv_copies(s, side):
        at = pl.ds(pl.multiple_of(s * shard, shard), shard)
        src, dst = ((rows - WIN, 0), (0, WIN + rows))[side]
        return [
            remote(
                hbm.at[pl.ds(src, WIN), at], ext.at[pl.ds(dst, WIN), at],
                kv_send.at[side, which, s], kv_recv.at[side, which, s], tm=(right, left)[side],
            )
            for which, (hbm, ext) in enumerate(((k_hbm, kext), (v_hbm, vext)))
        ]

    for i in range(n_dp):
        @pl.when(has_right)
        def _():
            for copy in kv_copies(turn(i), 0):
                copy.start()

        @pl.when(has_left)
        def _():
            for copy in kv_copies(turn(i), 1):
                copy.start()

    w_half = pl.ds(pl.multiple_of(core * half, half), half)
    w_copies = [
        remote(w_hbm.at[w_half], wfull.at[dp, w_half], w_send.at[k], w_recv.at[k], dp=peer(k + 1))
        for k in range(n_dp - 1)
    ]
    for copy in w_copies:
        copy.start()

    own[4].wait()
    length = len_ref[0]
    start = tm * rows
    row_pos = start + lax.broadcasted_iota(jnp.int32, (rows, 1), 0)
    valid = row_pos < length
    masked_grad = jnp.where(valid, g_ref[...].astype(F32), 0.0).astype(BF16)
    gm[...] = masked_grad
    gsplit[0] = masked_grad[:, :cols]
    gsplit[1] = masked_grad[:, cols:]
    g_copy = remote(gsplit.at[1 - core], gg.at[pl.ds(rows, rows)], g_send, g_recv, tm=partner)
    g_copy.start()
    gg[pl.ds(0, rows), :] = gsplit[core]

    @pl.when(jnp.logical_not(has_left))
    def _():
        kext[pl.ds(0, WIN), :] = jnp.zeros((WIN, width), BF16)
        vext[pl.ds(0, WIN), :] = jnp.zeros((WIN, width), BF16)
        halo_in[:, 1] = jnp.zeros((n_dp, 2, WIN, shard), BF16)

    @pl.when(jnp.logical_not(has_right))
    def _():
        kext[pl.ds(WIN + rows, WIN), :] = jnp.zeros((WIN, width), BF16)
        vext[pl.ds(WIN + rows, WIN), :] = jnp.zeros((WIN, width), BF16)
        halo_in[:, 0] = jnp.zeros((n_dp, 2, WIN, shard), BF16)

    for copy in own[:4]:
        copy.wait()

    span = rows + 2 * WIN
    q_pos = start + lax.broadcasted_iota(jnp.int32, (rows, span), 0)
    k_pos = start - WIN + lax.broadcasted_iota(jnp.int32, (rows, span), 1)
    allowed = (jnp.abs(q_pos - k_pos) <= WIN) & (k_pos >= 0) & (k_pos < length)
    bias = jnp.where(allowed, 0.0, NEG_FILL)
    live = jnp.where(valid, 1.0, 0.0)

    def ao_copy(s):
        return remote(
            ao.at[s, pl.ds(0, rows)], ao.at[s, pl.ds(rows, rows)], ao_send.at[s], ao_recv.at[s], tm=partner
        )

    def part_copy(c, k):
        return remote(
            part_out.at[c, k], part_in.at[c, k], p_send.at[c, k], p_recv.at[c, k], dp=peer(k + 1)
        )

    def send_part(k):
        s = peer(k + 1)
        ao_copy(s).wait_recv()
        for c in range(CHUNKS):
            part_out[c, k] = dot(ao[s], gg[:, c * ccols:(c + 1) * ccols], 0, 0).astype(BF16)
            part_copy(c, k).start()

    g_copy.wait_recv()

    @pl.loop(0, n_dp)
    def _(step):
        s = turn(step)

        @pl.when(has_left)
        def _():
            for copy in kv_copies(s, 0):
                copy.wait_recv()

        @pl.when(has_right)
        def _():
            for copy in kv_copies(s, 1):
                copy.wait_recv()

        at = pl.ds(pl.multiple_of(s * shard, shard), shard)
        q, k, v = q_ref[:, at], kext[:, at], vext[:, at]
        for i in range(heads):
            lanes = slice(i * head, (i + 1) * head)
            masked = dot(q[:, lanes], k[:, lanes], 1, 1) * scale + bias
            top = jnp.max(masked, axis=-1, keepdims=True)
            e = jnp.exp(masked - top)
            p = e * (live / jnp.sum(e, axis=-1, keepdims=True))
            probs[s * heads + i] = p
            ao[s, pl.ds(0, rows), lanes] = dot(p.astype(BF16), v[:, lanes], 1, 0).astype(BF16)
        ao_copy(s).start()

        @pl.when(step > 0)
        def _():
            send_part(step - 1)

    ao_copy(dp).wait_recv()
    for c in range(CHUNKS):
        acc[c] = dot(ao[dp], gg[:, c * ccols:(c + 1) * ccols], 0, 0)

    def w_copy(k):
        return remote(w_hbm.at[w_half], wfull.at[dp, w_half], w_send.at[k], w_recv.at[k], dp=peer(k + 1))

    def w_forward(k):
        src = lax.rem(dp + n_dp - 1 - k, n_dp)
        return remote(
            wfull.at[src, w_half], wfull.at[src, w_half], wf_send.at[k], wf_recv.at[k], tm=partner
        )

    def halo_copy(s, side):
        return remote(
            halo_out.at[s, side], halo_in.at[s, side], h_send.at[s, side], h_recv.at[s, side],
            tm=(left, right)[side],
        )

    @pl.loop(0, n_dp)
    def _(step):
        s = lax.rem(dp + n_dp - step, n_dp)

        @pl.when(step == 1)
        def _():
            for k in range(n_dp - 1):
                w_copy(k).wait_recv()
                w_forward(k).start()

        @pl.when(step > 0)
        def _():
            w_forward(step - 1).wait_recv()

        at = pl.ds(pl.multiple_of(s * shard, shard), shard)
        q, k, v = q_ref[:, at], kext[:, at], vext[:, at]
        grad_attn = dot(gm[...], wfull[s], 1, 1).astype(BF16)
        for i in range(heads):
            lanes = slice(i * head, (i + 1) * head)
            p = probs[s * heads + i]
            grad_probs = dot(grad_attn[:, lanes], v[:, lanes], 1, 1)
            delta = jnp.sum(p * grad_probs, axis=-1, keepdims=True)
            grad_scores = (p * (grad_probs - delta) * scale).astype(BF16)
            hd = pl.ds(pl.multiple_of(s * shard + i * head, head), head)
            dq_ref[:, hd] = dot(grad_scores, k[:, lanes], 1, 0).astype(BF16)
            terms = (
                dot(grad_scores, q[:, lanes], 0, 0),
                dot(p.astype(BF16), grad_attn[:, lanes], 0, 0),
            )
            for which, term in enumerate(terms):
                halo_out[s, 0, which, :, lanes] = term[:WIN].astype(BF16)
                halo_out[s, 1, which, :, lanes] = term[WIN + rows:].astype(BF16)
                mids[which, :, hd] = term[WIN:WIN + rows]

        @pl.when(has_left)
        def _():
            halo_copy(s, 0).start()

        @pl.when(has_right)
        def _():
            halo_copy(s, 1).start()

    def z_copy(c, k):
        return remote(
            z_out.at[c, z_peer(k + 1)], z_in.at[c, k], z_send.at[c, k], z_recv.at[c, k],
            tm=2 * z_peer(k + 1) + core,
        )

    def final_copy(c, k):
        return remote(
            final.at[core, c, z], final.at[core, c, z], f_send.at[c, k], f_recv.at[c, k],
            tm=2 * z_peer(k + 1) + core,
        )

    def cross_copy(c):
        return remote(final.at[core, c], final.at[core, c], x_send.at[c], x_recv.at[c], tm=partner)

    def cut(j):
        r, a = (j // across) * prow, (j % across) * pcol
        return slice(r, r + prow), slice(a, a + pcol)

    def scatter(c):
        total = acc[c]
        for k in range(n_dp - 1):
            part_copy(c, k).wait_recv()
            total = total + part_in[c, k].astype(F32)
        for j in range(nz):
            r, a = cut(j)
            z_own[c, j] = total[r, a]
            z_out[c, j] = total[r, a].astype(BF16)
        for k in range(nz - 1):
            z_copy(c, k).start()

    def gather(c):
        total = z_own[c, z]
        for k in range(nz - 1):
            z_copy(c, k).wait_recv()
            total = total + z_in[c, k].astype(F32)
        final[core, c, z] = (total * inv_count).astype(BF16)
        for k in range(nz - 1):
            final_copy(c, k).start()

    def cross(c):
        for k in range(nz - 1):
            final_copy(c, k).wait_recv()
        cross_copy(c).start()

    for c in range(CHUNKS):
        scatter(c)

    attended = dot(ao[0, pl.ds(0, rows)], wfull[0], 1, 0)
    for s in range(1, n_dp):
        attended += dot(ao[s, pl.ds(0, rows)], wfull[s], 1, 0)
    att_ref[...] = jnp.where(valid, attended, 0.0).astype(BF16)

    for c in range(CHUNKS):
        gather(c)

    @pl.when(has_right)
    def _():
        for s in range(n_dp):
            halo_copy(s, 0).wait_recv()

    @pl.when(has_left)
    def _():
        for s in range(n_dp):
            halo_copy(s, 1).wait_recv()

    for which, out in enumerate((dk_ref, dv_ref)):
        for s in range(n_dp):
            lanes = slice(s * shard, (s + 1) * shard)
            out[0:WIN, lanes] = (
                mids[which, 0:WIN, lanes] + halo_in[s, 1, which].astype(F32)
            ).astype(BF16)
            if rows > 2 * WIN:
                out[WIN:rows - WIN, lanes] = mids[which, WIN:rows - WIN, lanes].astype(BF16)
            out[rows - WIN:rows, lanes] = (
                mids[which, rows - WIN:rows, lanes] + halo_in[s, 0, which].astype(F32)
            ).astype(BF16)

    for c in range(CHUNKS):
        cross(c)
    for c in range(CHUNKS):
        cross_copy(c).wait_recv()
    for side in range(2):
        for c in range(CHUNKS):
            for j in range(nz):
                r, a = cut(j)
                base = side * cols + c * ccols
                gw_ref[r, base + a.start:base + a.stop] = final[side, c, j]

    @pl.when(has_right)
    def _():
        for s in range(n_dp):
            for copy in kv_copies(s, 0):
                copy.wait_send()
            halo_copy(s, 1).wait_send()

    @pl.when(has_left)
    def _():
        for s in range(n_dp):
            for copy in kv_copies(s, 1):
                copy.wait_send()
            halo_copy(s, 0).wait_send()

    g_copy.wait_send()
    for k in range(n_dp - 1):
        w_copies[k].wait_send()
        w_forward(k).wait_send()
    for s in range(n_dp):
        ao_copy(s).wait_send()
    for c in range(CHUNKS):
        for k in range(n_dp - 1):
            part_copy(c, k).wait_send()
        for k in range(nz - 1):
            z_copy(c, k).wait_send()
            final_copy(c, k).wait_send()
        cross_copy(c).wait_send()


def hand_over_kernel(count, *refs):
    srcs, dsts, held = refs[:count], refs[count:2 * count], refs[2 * count:3 * count]
    wide, sem_in, sem_out = refs[3 * count:]
    loads, stores = [], []
    for i in range(count):
        part = srcs[i].shape[0] // PARTS
        for j in range(PARTS):
            at = pl.ds(j * part, part)
            loads.append(pltpu.make_async_copy(srcs[i].at[at], held[i].at[at], sem_in.at[i, j]))
            ready = wide if i == count - 1 else held[i]
            stores.append(pltpu.make_async_copy(ready.at[at], dsts[i].at[at], sem_out.at[i, j]))
    for load in loads:
        load.start()
    for n, (load, store) in enumerate(zip(loads, stores)):
        load.wait()
        if n >= (count - 1) * PARTS:
            at = pl.ds((n - (count - 1) * PARTS) * part, part)
            wide[at, :] = held[-1][at, :].astype(F32)
        store.start()
    for store in stores:
        store.wait()


def hand_over(arrays):
    hbm = pl.BlockSpec(memory_space=pl.ANY)
    return pl.pallas_call(
        functools.partial(hand_over_kernel, len(arrays)),
        out_shape=tuple(jax.ShapeDtypeStruct(a.shape, a.dtype) for a in arrays[:-1])
        + (jax.ShapeDtypeStruct(arrays[-1].shape, F32),),
        in_specs=[hbm] * len(arrays),
        out_specs=(hbm,) * len(arrays),
        scratch_shapes=[pltpu.VMEM(a.shape, a.dtype) for a in arrays]
        + [pltpu.VMEM(arrays[-1].shape, F32)]
        + [pltpu.SemaphoreType.DMA((len(arrays), PARTS))] * 2,
        compiler_params=pltpu.CompilerParams(vmem_limit_bytes=60 * 1024 * 1024),
    )(*arrays)


def per_device(queries, keys, values, lengths, out_weight, grad_out):
    n_tm = lax.axis_size("tm")
    n_dp = lax.axis_size("dp")
    rows, width = queries.shape[1:]
    shard = width // n_dp
    span = rows + 2 * WIN
    nz = n_tm // 2
    cols = width // 2
    ccols = cols // CHUNKS
    _, _, prow, pcol = piece_grid(nz, shard, ccols)
    inv_count = 1.0 / math.sqrt(n_dp * rows * n_tm)
    vmem = pl.BlockSpec(memory_space=pltpu.VMEM)
    hbm = pl.BlockSpec(memory_space=pl.ANY)
    dma = pltpu.SemaphoreType.DMA
    block = jax.ShapeDtypeStruct((rows, width), BF16)
    outs = pl.pallas_call(
        functools.partial(kernel, n_tm, n_dp, inv_count),
        out_shape=(block, block, block, block, jax.ShapeDtypeStruct((shard, width), BF16)),
        in_specs=[pl.BlockSpec(memory_space=pltpu.SMEM), hbm, hbm, hbm, hbm, hbm],
        out_specs=(vmem,) * 5,
        scratch_shapes=[
            pltpu.VMEM((rows, width), BF16),
            pltpu.VMEM((rows, width), BF16),
            pltpu.VMEM((span, width), BF16),
            pltpu.VMEM((span, width), BF16),
            pltpu.VMEM((n_dp, shard, width), BF16),
            pltpu.VMEM((rows, width), BF16),
            pltpu.VMEM((2, rows, cols), BF16),
            pltpu.VMEM((2 * rows, cols), BF16),
            pltpu.VMEM((n_dp, 2 * rows, shard), BF16),
            pltpu.VMEM((H, rows, span), F32),
            pltpu.VMEM((2, rows, width), F32),
            pltpu.VMEM((n_dp, 2, 2, WIN, shard), BF16),
            pltpu.VMEM((n_dp, 2, 2, WIN, shard), BF16),
            pltpu.VMEM((CHUNKS, n_dp - 1, shard, ccols), BF16),
            pltpu.VMEM((CHUNKS, n_dp - 1, shard, ccols), BF16),
            pltpu.VMEM((CHUNKS, shard, ccols), F32),
            pltpu.VMEM((CHUNKS, nz, prow, pcol), F32),
            pltpu.VMEM((CHUNKS, nz, prow, pcol), BF16),
            pltpu.VMEM((CHUNKS, nz - 1, prow, pcol), BF16),
            pltpu.VMEM((2, CHUNKS, nz, prow, pcol), BF16),
            dma((5,)),
            dma((2, 2, n_dp)), dma((2, 2, n_dp)),
            dma((n_dp - 1,)), dma((n_dp - 1,)),
            dma((n_dp - 1,)), dma((n_dp - 1,)),
            dma(()), dma(()),
            dma((n_dp,)), dma((n_dp,)),
            dma((n_dp, 2)), dma((n_dp, 2)),
            dma((CHUNKS, n_dp - 1)), dma((CHUNKS, n_dp - 1)),
            dma((CHUNKS, nz - 1)), dma((CHUNKS, nz - 1)),
            dma((CHUNKS, nz - 1)), dma((CHUNKS, nz - 1)),
            dma((CHUNKS,)), dma((CHUNKS,)),
        ],
        compiler_params=pltpu.CompilerParams(
            collective_id=0, has_side_effects=True, vmem_limit_bytes=60 * 1024 * 1024
        ),
        cost_estimate=pl.CostEstimate(flops=4_000_000_000, bytes_accessed=8_000_000, transcendentals=1_000_000),
    )(lengths, queries[0], keys[0], values[0], out_weight, grad_out[0])
    attended, dq, dk, dv, gw = hand_over(outs)
    return (attended[None], dq[None], dk[None], dv[None], gw)


def solution(mesh):
    frames = P(("groups", "dp"), "tm", None)
    return jax.shard_map(
        per_device,
        mesh=mesh,
        in_specs=(frames, frames, frames, P(("groups", "dp")), P("dp", None), frames),
        out_specs=(frames, frames, frames, frames, P(("groups", "dp"), None)),
        check_vma=False,
    )
```
